32 devices in a mesh: row: 4 (over y, core), col: 4 (over z), depth: 2 (over x).
Axes of the slice: x: 2, y: 2, z: 4, core: 2. Of those that a mesh axis runs over, the one named last changes fastest.
Arguments:
- tokens: bfloat16 [4096, 2048], P(('depth', 'row'), 'col'), may hold values from -6 to 6
- w_in: bfloat16 [8192, 2048], P('col', 'row'), may hold values from -0.125 to 0.125
- w_out: bfloat16 [2048, 8192], P('row', 'col'), may hold values from -0.0625 to 0.0625
- grad_out: bfloat16 [4096, 2048], P(('depth', 'row'), 'col'), may hold values from -6 to 6
Outputs:
- output: bfloat16 [4096, 2048], P(('depth', 'row'), 'col')
- grad_tokens: bfloat16 [4096, 2048], P(('depth', 'row'), 'col')
- grad_w_in: bfloat16 [8192, 2048], P('col', 'row')
- grad_w_out: bfloat16 [2048, 8192], P('row', 'col')
The draws below stay inside these ranges and needn't reach their ends.
All inputs are finite; a program needn't handle non-finite values.
Results may differ from the reference program's by a relative error of at most 0.005.
Values may be sent and summed in bfloat16 or wider, within the bound.
A program may use at most 192 MiB of HBM per device.

```python
import math
import jax
import jax.numpy as jnp
from jax import lax

D = 2048
H = 8192
TOKENS = 4096


def with_spikes(array, own_key, source, target, blocks, factor):
    owner, partner = [(jnp.arange(array.shape[position]) // (array.shape[position] // blocks)).reshape([-1 if axis == position else 1 for axis in range(array.ndim)]) for position in (source, target)]
    chosen = jax.random.permutation(own_key, blocks)[partner]
    strong = (owner == chosen) | (owner == (partner + blocks // 2) % blocks)
    return jnp.where(strong, factor * array, array)


def block_levels(key, shape, pieces, low, high):
    def one(axis_at, parts):
        heights = jax.random.uniform(jax.random.fold_in(jax.random.fold_in(key, 6), axis_at), (parts,), jnp.float32, low / len(pieces), high / len(pieces))
        return jnp.repeat(jnp.exp(heights), shape[axis_at] // parts).reshape((-1,) + (1,) * (len(shape) - axis_at - 1))

    gain = one(*pieces[0])
    for cut in pieces[1:]:
        gain = gain * one(*cut)
    return gain


def normal_values(key, dims, width, most, shards=(), kind=jnp.bfloat16):
    values = width * jax.random.normal(key, dims, jnp.float32)
    if shards:
        values = values * block_levels(key, dims, shards, -0.22, 0.18)
    return jnp.clip(values, -most, most).astype(kind)


def heavy_noise(stream_key, extent, scale, reach, pieces, heavy, kind=jnp.bfloat16):
    drawn = scale * jax.random.normal(stream_key, extent, jnp.float32)
    if pieces:
        drawn = drawn * block_levels(stream_key, extent, pieces, -0.22, 0.18)
    return jnp.clip(with_spikes(drawn, jax.random.fold_in(stream_key, 3), *heavy), -reach, reach).astype(kind)


def setup_inputs(seed: int = 0) -> dict:
    arg_keys = jax.random.split(jax.random.key(seed), 5)
    return {
        "tokens": heavy_noise(arg_keys[0], (TOKENS, D), 1.0, 6.0, ((0, 8), (1, 4)), (0, 1, 8, 2.0)),
        "w_in": normal_values(arg_keys[1], (H, D), D ** -0.5, 0.125, ((0, 4), (1, 4))),
        "w_out": normal_values(arg_keys[2], (D, H), H ** -0.5, 0.0625, ((0, 4), (1, 4))),
        "grad_out": heavy_noise(arg_keys[3], (TOKENS, D), 1.0, 6.0, ((0, 8), (1, 4)), (0, 1, 8, 2.0)),
    }


def gelu_value(pre):
    return 0.5 * pre * (1.0 + lax.erf(pre / math.sqrt(2.0)))

def gelu_slope(pre):
    return 0.5 * (1.0 + lax.erf(pre / math.sqrt(2.0))) + pre * jnp.exp(-0.5 * pre * pre) / math.sqrt(2.0 * math.pi)

def reference(tokens, w_in, w_out, grad_out):
    pre = jnp.dot(tokens, w_in.T, preferred_element_type=jnp.float32)
    act = gelu_value(pre).astype(jnp.bfloat16)
    output = jnp.dot(act, w_out.T, preferred_element_type=jnp.float32).astype(jnp.bfloat16)
    d_act = jnp.dot(grad_out, w_out, preferred_element_type=jnp.float32)
    d_pre = (d_act * gelu_slope(pre)).astype(jnp.bfloat16)
    grad_tokens = jnp.dot(d_pre, w_in, preferred_element_type=jnp.float32).astype(jnp.bfloat16)
    factor = 1.0 / math.sqrt(TOKENS)
    grad_w_out = (jnp.dot(grad_out.T, act, preferred_element_type=jnp.float32) * factor).astype(jnp.bfloat16)
    grad_w_in = (jnp.dot(d_pre.T, tokens, preferred_element_type=jnp.float32) * factor).astype(jnp.bfloat16)
    return (output, grad_tokens, grad_w_in, grad_w_out)
```

```python
import functools
import math

import jax
import jax.numpy as jnp
from jax import lax
from jax.experimental import pallas as pl
from jax.experimental.pallas import tpu as pltpu
from jax.sharding import PartitionSpec as P

F32 = jnp.float32
BF16 = jnp.bfloat16
MESH = pl.DeviceIdType.MESH
ROWS = 32


def mm(left, right, ldim, rdim):
    return lax.dot_general(
        left, right, (((ldim,), (rdim,)), ((), ())), preferred_element_type=F32
    )


def wide(x):
    return x.astype(F32)


def kernel(
    nz, nd, fac,
    tok_in, win_in, wout_in, cot_in,
    out_ref, gtok_ref, gwin_ref, gwout_ref,
    tok, cot, win, wout, slope, act, dpre,
    psend, own, crecv, yrecv, xrecv, osend, orecv,
    loc_sem, zs, zr, as_, ar, cs, cr, ys, yr, xs, xr, os_, or_, fin_sem,
):
    T, D = tok.shape
    H = win.shape[0]
    bz, br = D // nz, D // 4
    hc = own.shape[3]
    nq = H // hc
    r = lax.axis_index("row")
    z = lax.axis_index("col")
    d = lax.axis_index("depth")
    c, y = lax.rem(r, 2), r // 2
    cp = y * 2 + (1 - c)
    yp = (1 - y) * 2 + c

    bar = pltpu.get_barrier_semaphore()
    for k in range(1, nz):
        pl.semaphore_signal(bar, inc=1, device_id={"col": lax.rem(z + k, nz)}, device_id_type=MESH)
    for k in range(1, nd):
        pl.semaphore_signal(bar, inc=1, device_id={"depth": lax.rem(d + k, nd)}, device_id_type=MESH)
    pl.semaphore_signal(bar, inc=1, device_id={"row": cp}, device_id_type=MESH)
    pl.semaphore_signal(bar, inc=1, device_id={"row": yp}, device_id_type=MESH)
    pl.semaphore_wait(bar, nz + nd)

    def send(src, dst, ss, rs, who):
        return pltpu.make_async_remote_copy(
            src_ref=src, dst_ref=dst, send_sem=ss, recv_sem=rs, device_id=who, device_id_type=MESH
        )

    def zcol(ref, i):
        return ref.at[:, pl.ds(pl.multiple_of(i * bz, bz), bz)]

    def wblk(a, i):
        at = pl.ds(pl.multiple_of(i * br, br), br)
        return win.at[:, at] if a == 0 else wout.at[at, :]

    acts_in, acts = (tok_in, cot_in), (tok, cot)
    w_in = (win_in, wout_in)

    def zcopy(a, k):
        return send(acts_in[a], zcol(acts[a], z), zs.at[a, k - 1], zr.at[a, k - 1], {"col": lax.rem(z + k, nz)})

    def ycopy(a):
        return send(w_in[a], wblk(a, r), as_.at[a, 0], ar.at[a, 0], {"row": yp})

    def ccopy(a):
        return send(w_in[a], wblk(a, r), as_.at[a, 1], ar.at[a, 1], {"row": cp})

    def fcopy(a):
        return send(wblk(a, yp), wblk(a, yp), as_.at[a, 2], ar.at[a, 2], {"row": cp})

    def lcopies(a):
        return (
            pltpu.make_async_copy(acts_in[a], zcol(acts[a], z), loc_sem.at[a, 0]),
            pltpu.make_async_copy(w_in[a], wblk(a, r), loc_sem.at[a, 1]),
        )

    for a in range(2):
        ycopy(a).start()
        for k in range(1, nz):
            zcopy(a, k).start()
        ccopy(a).start()
        for x in lcopies(a):
            x.start()

    def wait_acts(a):
        lcopies(a)[0].wait()
        for k in range(1, nz):
            zcopy(a, k).wait()

    def wait_weights(a):
        ycopy(a).wait()
        fcopy(a).start()
        lcopies(a)[1].wait()
        ccopy(a).wait()
        fcopy(a).wait()

    def hsl(q):
        return pl.ds(pl.multiple_of(q * hc, hc), hc)

    def rsl(i):
        return pl.ds(pl.multiple_of(i * ROWS, ROWS), ROWS)

    wait_acts(0)
    wait_weights(0)

    @pl.loop(0, nq)
    def _(q):
        slope[:, hsl(q)] = mm(tok[...], win[hsl(q), :], 1, 1)

        @pl.loop(0, T // ROWS)
        def _(i):
            v = slope[rsl(i), hsl(q)]
            half = 0.5 * (1.0 + lax.erf(v * (1.0 / math.sqrt(2.0))))
            act[rsl(i), hsl(q)] = (v * half).astype(BF16)
            slope[rsl(i), hsl(q)] = half + v * jnp.exp(-0.5 * v * v) * (1.0 / math.sqrt(2.0 * math.pi))

    def core_copy(u, slot):
        return send(psend.at[slot], crecv.at[u], cs.at[slot], cr.at[u], {"row": cp})

    def y_copy(u):
        return send(own.at[u, 1 - y], yrecv.at[u], ys.at[u], yr.at[u], {"row": yp})

    def ufinal(u):
        return own.at[u, y] if nd == 2 else xrecv.at[u, d]

    def x_copy(u, k):
        dst = xrecv.at[u, 0] if nd == 2 else xrecv.at[u, d]
        return send(ufinal(u), dst, xs.at[u, k - 1], xr.at[u, k - 1], {"depth": lax.rem(d + k, nd)})

    def fold(u):
        core_copy(u, lax.rem(u, 2)).wait_recv()

        @pl.loop(0, hc // ROWS)
        def _(i):
            own[u, 1 - y, rsl(i), :] = (
                wide(own[u, 1 - y, rsl(i), :]) + wide(crecv[u, 1 - y, rsl(i), :])
            ).astype(BF16)

        y_copy(u).start()

    def fold_rows(u):
        y_copy(u).wait_recv()
        dst = ufinal(u)

        @pl.loop(0, hc // ROWS)
        def _(i):
            dst[rsl(i), :] = (
                wide(own[u, y, rsl(i), :]) + wide(crecv[u, y, rsl(i), :]) + wide(yrecv[u, rsl(i), :])
            ).astype(BF16)

        for k in range(1, nd):
            x_copy(u, k).start()

    def final_copy(a, q):
        u = a * nq + q
        dst = gwout_ref.at[:, hsl(q)] if a == 0 else gwin_ref.at[hsl(q), :]
        return pltpu.make_async_copy(yrecv.at[u], dst, fin_sem.at[u])

    def finish(a, q):
        u = a * nq + q
        for k in range(1, nd):
            x_copy(u, k).wait_recv()

        @pl.loop(0, hc // ROWS)
        def _(i):
            if nd == 2:
                total = wide(own[u, y, rsl(i), :]) + wide(xrecv[u, 0, rsl(i), :])
            else:
                total = wide(xrecv[u, 0, rsl(i), :])
                for e in range(1, nd):
                    total = total + wide(xrecv[u, e, rsl(i), :])
            yrecv[u, rsl(i), :] = (total * fac).astype(BF16)

        final_copy(a, q).start()

    def produce(a):
        left_all = cot if a == 0 else tok

        @pl.loop(0, nq)
        def _(q):
            u = a * nq + q
            slot = lax.rem(u, 2)

            @pl.when(u >= 2)
            def _():
                core_copy(u, slot).wait_send()

            for mine in range(2):
                for yy in range(2):
                    owner = yy * 2 + (c if mine else 1 - c)
                    feats = left_all[:, pl.ds(pl.multiple_of(owner * br, br), br)]
                    if a == 0:
                        tile = mm(feats, act[:, hsl(q)], 0, 0)
                    else:
                        tile = mm(dpre[:, hsl(q)], feats, 0, 0)
                    if mine:
                        own[u, yy] = tile.astype(BF16)
                    else:
                        psend[slot, yy] = tile.astype(BF16)
                if not mine:
                    core_copy(u, slot).start()

            @pl.when(u >= 1)
            def _():
                fold(u - 1)

    def out_copy(a, k):
        return send(osend.at[a, k - 1], orecv.at[a, k - 1], os_.at[a, k - 1], or_.at[a, k - 1], {"col": lax.rem(z + k, nz)})

    def terms(a):
        for k in range(1, nz + 1):
            to = lax.rem(z + k, nz)
            at = pl.ds(pl.multiple_of(to * bz, bz), bz)
            term = mm(act[...], wout[at, :], 1, 1) if a == 0 else mm(dpre[...], win[:, at], 1, 0)
            if k < nz:
                osend[a, k - 1] = term.astype(BF16)
                out_copy(a, k).start()
            else:
                slope[:, a * bz : (a + 1) * bz] = term

    wait_acts(1)
    produce(0)
    wait_weights(1)

    @pl.loop(0, nq)
    def _(q):
        slope[:, hsl(q)] = slope[:, hsl(q)] * mm(cot[...], wout[:, hsl(q)], 1, 0)
        dpre[:, hsl(q)] = slope[:, hsl(q)].astype(BF16)

    produce(1)
    fold(2 * nq - 1)
    terms(0)
    terms(1)

    total_units = 2 * nq

    def drain(a):
        @pl.loop(0, nq)
        def _(q):
            u = a * nq + q
            fold_rows(u)
            if a == 1:
                finish(0, q)

    drain(0)
    drain(1)

    def out_final(a):
        return pltpu.make_async_copy(orecv.at[a, 0], (out_ref, gtok_ref)[a], fin_sem.at[total_units + a])

    for a in range(2):
        for k in range(1, nz):
            out_copy(a, k).wait()

        @pl.loop(0, T // ROWS)
        def _(i):
            total = slope[rsl(i), a * bz : (a + 1) * bz]
            for k in range(1, nz):
                total = total + wide(orecv[a, k - 1, rsl(i), :])
            orecv[a, 0, rsl(i), :] = total.astype(BF16)

        out_final(a).start()

    @pl.loop(0, nq)
    def _(q):
        finish(1, q)

    for s in range(2):
        core_copy(total_units - 2 + s, (total_units - 2 + s) % 2).wait_send()

    for a in range(2):
        out_final(a).wait()

        @pl.loop(0, nq)
        def _(q):
            u = a * nq + q
            y_copy(u).wait_send()
            for k in range(1, nd):
                x_copy(u, k).wait_send()
            final_copy(a, q).wait()


def local(nz, nd, tokens, w_in, w_out, grad_out):
    T, bz = tokens.shape
    D = bz * nz
    H = w_in.shape[0]
    br = w_in.shape[1]
    hc = br
    nq = H // hc
    nx = 1 if nd == 2 else nd
    fac = 1.0 / math.sqrt(T * 4 * nd)
    dma = pltpu.SemaphoreType.DMA
    anyspec = pl.BlockSpec(memory_space=pl.ANY)
    flops = 12 * T * D * H
    return pl.pallas_call(
        functools.partial(kernel, nz, nd, fac),
        out_shape=(
            jax.ShapeDtypeStruct((T, bz), BF16),
            jax.ShapeDtypeStruct((T, bz), BF16),
            jax.ShapeDtypeStruct((H, br), BF16),
            jax.ShapeDtypeStruct((br, H), BF16),
        ),
        in_specs=[anyspec] * 4,
        out_specs=(anyspec,) * 4,
        scratch_shapes=[
            pltpu.VMEM((T, D), BF16),
            pltpu.VMEM((T, D), BF16),
            pltpu.VMEM((H, D), BF16),
            pltpu.VMEM((D, H), BF16),
            pltpu.VMEM((T, H), F32),
            pltpu.VMEM((T, H), BF16),
            pltpu.VMEM((T, H), BF16),
            pltpu.VMEM((2, 2, hc, br), BF16),
            pltpu.VMEM((2 * nq, 2, hc, br), BF16),
            pltpu.VMEM((2 * nq, 2, hc, br), BF16),
            pltpu.VMEM((2 * nq, hc, br), BF16),
            pltpu.VMEM((2 * nq, nx, hc, br), BF16),
            pltpu.VMEM((2, nz - 1, T, bz), BF16),
            pltpu.VMEM((2, nz - 1, T, bz), BF16),
            dma((2, 2)),
            dma((2, nz - 1)),
            dma((2, nz - 1)),
            dma((2, 3)),
            dma((2, 3)),
            dma((2,)),
            dma((2 * nq,)),
            dma((2 * nq,)),
            dma((2 * nq,)),
            dma((2 * nq, max(nd - 1, 1))),
            dma((2 * nq, max(nd - 1, 1))),
            dma((2, nz - 1)),
            dma((2, nz - 1)),
            dma((2 * nq + 2,)),
        ],
        compiler_params=pltpu.CompilerParams(
            collective_id=0, has_side_effects=True, vmem_limit_bytes=VMEM_LIMIT
        ),
        cost_estimate=pl.CostEstimate(flops=flops, bytes_accessed=20 * 2**20, transcendentals=2 * T * H),
        name="mlp",
    )(tokens, w_in, w_out, grad_out)


VMEM_LIMIT = 64 * 2**20 - 2**16


def solution(mesh):
    nz, nd = mesh.shape["col"], mesh.shape["depth"]
    in_specs = (
        P(("depth", "row"), "col"),
        P("col", "row"),
        P("row", "col"),
        P(("depth", "row"), "col"),
    )
    out_specs = (
        P(("depth", "row"), "col"),
        P(("depth", "row"), "col"),
        P("col", "row"),
        P("row", "col"),
    )
    return jax.shard_map(
        functools.partial(local, nz, nd), mesh=mesh, in_specs=in_specs, out_specs=out_specs, check_vma=False
    )
```

```python
import functools
import math

import jax
import jax.numpy as jnp
from jax import lax
from jax.experimental import pallas as pl
from jax.experimental.pallas import tpu as pltpu
from jax.sharding import PartitionSpec as P

F32 = jnp.float32
BF16 = jnp.bfloat16
MESH = pl.DeviceIdType.MESH
ROWS = 32


def mm(left, right, ldim, rdim):
    return lax.dot_general(
        left, right, (((ldim,), (rdim,)), ((), ())), preferred_element_type=F32
    )


def wide(x):
    return x.astype(F32)


def kernel(
    nz, nd, fac,
    tok_in, win_in, wout_in, cot_in,
    out_ref, gtok_ref, gwin_ref, gwout_ref,
    tok, cot, win, wout, slope, act, dpre,
    psend, own, crecv, yrecv, xrecv, osend, orecv, mine_f32,
    loc_sem, zs, zr, as_, ar, cs, cr, ys, yr, xs, xr, os_, or_, fin_sem,
):
    T, D = tok.shape
    H = win.shape[0]
    bz, br = D // nz, D // 4
    hc = own.shape[3]
    nq = H // hc
    r = lax.axis_index("row")
    z = lax.axis_index("col")
    d = lax.axis_index("depth")
    c, y = lax.rem(r, 2), r // 2
    cp = y * 2 + (1 - c)
    yp = (1 - y) * 2 + c

    bar = pltpu.get_barrier_semaphore()
    for k in range(1, nz):
        pl.semaphore_signal(bar, inc=1, device_id={"col": lax.rem(z + k, nz)}, device_id_type=MESH)
    for k in range(1, nd):
        pl.semaphore_signal(bar, inc=1, device_id={"depth": lax.rem(d + k, nd)}, device_id_type=MESH)
    pl.semaphore_signal(bar, inc=1, device_id={"row": cp}, device_id_type=MESH)
    pl.semaphore_signal(bar, inc=1, device_id={"row": yp}, device_id_type=MESH)
    pl.semaphore_wait(bar, nz + nd)

    def send(src, dst, ss, rs, who):
        return pltpu.make_async_remote_copy(
            src_ref=src, dst_ref=dst, send_sem=ss, recv_sem=rs, device_id=who, device_id_type=MESH
        )

    def zcol(ref, i):
        return ref.at[:, pl.ds(pl.multiple_of(i * bz, bz), bz)]

    def wblk(a, i):
        at = pl.ds(pl.multiple_of(i * br, br), br)
        return win.at[:, at] if a == 0 else wout.at[at, :]

    acts_in, acts = (tok_in, cot_in), (tok, cot)
    w_in = (win_in, wout_in)

    def zhop(a, way, s):
        shard = z - s if way == 0 else z + s
        to = lax.rem(z + (1 if way == 0 else nz - 1), nz)
        src = acts_in[a] if s == 0 else zcol(acts[a], shard)
        return send(src, zcol(acts[a], shard), zs.at[a, way, s], zr.at[a, way, s], {"col": to})

    def sends(way, s):
        if way == 0:
            return jnp.logical_and(z >= s, z < nz - 1)
        return jnp.logical_and(z < nz - s, z > 0)

    def gets(way, s):
        return z >= s + 1 if way == 0 else z < nz - 1 - s

    def zstart(a, s):
        for way in range(2):
            pl.when(sends(way, s))(lambda way=way: zhop(a, way, s).start())

    def zwait(a, s):
        for way in range(2):
            pl.when(gets(way, s))(lambda way=way: zhop(a, way, s).wait_recv())

    def zdone(a):
        for s in range(nz - 1):
            for way in range(2):
                pl.when(sends(way, s))(lambda way=way, s=s: zhop(a, way, s).wait_send())

    def part(a, shard, e):
        if a == 0:
            n = H // nd
            return win.at[
                pl.ds(pl.multiple_of(e * n, n), n), pl.ds(pl.multiple_of(shard * br, br), br)
            ]
        n = br // nd
        return wout.at[pl.ds(pl.multiple_of(shard * br + e * n, n), n), :]

    def ycopy(a):
        n = (H if a == 0 else br) // nd
        src = w_in[a].at[pl.ds(pl.multiple_of(d * n, n), n), :]
        return send(src, part(a, r, d), as_.at[a, 0], ar.at[a, 0], {"row": yp})

    def ccopy(a):
        return send(w_in[a], wblk(a, r), as_.at[a, 1], ar.at[a, 1], {"row": cp})

    def dcopy(a, k):
        p = part(a, yp, d)
        return send(p, p, as_.at[a, 1 + k], ar.at[a, 1 + k], {"depth": lax.rem(d + k, nd)})

    def fcopy(a, k):
        p = part(a, yp, lax.rem(d + nd - k, nd))
        return send(p, p, as_.at[a, 1 + nd + k], ar.at[a, 1 + nd + k], {"row": cp})

    def lcopies(a):
        return (
            pltpu.make_async_copy(acts_in[a], zcol(acts[a], z), loc_sem.at[a, 0]),
            pltpu.make_async_copy(w_in[a], wblk(a, r), loc_sem.at[a, 1]),
        )

    def weights_hop(a):
        ycopy(a).wait_recv()
        for k in range(1, nd):
            dcopy(a, k).start()
        fcopy(a, 0).start()

    def weights_end(a):
        for k in range(1, nd):
            dcopy(a, k).wait_recv()
            fcopy(a, k).start()
        lcopies(a)[1].wait()
        ccopy(a).wait()
        ycopy(a).wait_send()
        for k in range(1, nd):
            dcopy(a, k).wait_send()
        for k in range(nd):
            fcopy(a, k).wait()

    ycopy(0).start()
    zstart(0, 0)
    for a in range(2):
        ccopy(a).start()
        for x in lcopies(a):
            x.start()
    zwait(0, 0)
    if nz > 2:
        zstart(0, 1)
    weights_hop(0)
    ycopy(1).start()
    for s in range(2, nz - 1):
        zwait(0, s - 1)
        zstart(0, s)
    zstart(1, 0)
    if nz > 2:
        zwait(0, nz - 2)
    lcopies(0)[0].wait()
    weights_end(0)

    def cot_hop(s):
        zwait(1, s - 1)
        zstart(1, s)

    hooks = [functools.partial(cot_hop, s) for s in range(1, nz - 1)]
    hooks.insert(1, functools.partial(weights_hop, 1))

    def hsl(q):
        return pl.ds(pl.multiple_of(q * hc, hc), hc)

    def rsl(i):
        return pl.ds(pl.multiple_of(i * ROWS, ROWS), ROWS)

    @pl.loop(0, nq)
    def _(q):
        for i, hook in enumerate(hooks[:nq]):
            pl.when(q == i)(hook)
        slope[:, hsl(q)] = mm(tok[...], win[hsl(q), :], 1, 1)

        @pl.loop(0, T // ROWS)
        def _(i):
            v = slope[rsl(i), hsl(q)]
            half = 0.5 * (1.0 + lax.erf(v * (1.0 / math.sqrt(2.0))))
            act[rsl(i), hsl(q)] = (v * half).astype(BF16)
            slope[rsl(i), hsl(q)] = half + v * jnp.exp(-0.5 * v * v) * (1.0 / math.sqrt(2.0 * math.pi))

    def core_copy(u, slot):
        return send(psend.at[slot], crecv.at[u], cs.at[slot], cr.at[u], {"row": cp})

    def y_copy(u):
        return send(own.at[u, 1 - y], yrecv.at[u], ys.at[u], yr.at[u], {"row": yp})

    def ufinal(u):
        return own.at[u, y] if nd == 2 else xrecv.at[u, d]

    def x_copy(u, k):
        dst = xrecv.at[u, 0] if nd == 2 else xrecv.at[u, d]
        return send(ufinal(u), dst, xs.at[u, k - 1], xr.at[u, k - 1], {"depth": lax.rem(d + k, nd)})

    def fold(u):
        core_copy(u, lax.rem(u, 2)).wait_recv()

        @pl.loop(0, hc // ROWS)
        def _(i):
            own[u, 1 - y, rsl(i), :] = (
                wide(own[u, 1 - y, rsl(i), :]) + wide(crecv[u, 1 - y, rsl(i), :])
            ).astype(BF16)

        y_copy(u).start()

    def fold_rows(u):
        y_copy(u).wait_recv()
        dst = ufinal(u)

        @pl.loop(0, hc // ROWS)
        def _(i):
            dst[rsl(i), :] = (
                wide(own[u, y, rsl(i), :]) + wide(crecv[u, y, rsl(i), :]) + wide(yrecv[u, rsl(i), :])
            ).astype(BF16)

        for k in range(1, nd):
            x_copy(u, k).start()

    def final_copy(a, q):
        u = a * nq + q
        dst = gwout_ref.at[:, hsl(q)] if a == 0 else gwin_ref.at[hsl(q), :]
        return pltpu.make_async_copy(yrecv.at[u], dst, fin_sem.at[u])

    def finish(a, q):
        u = a * nq + q
        for k in range(1, nd):
            x_copy(u, k).wait_recv()

        @pl.loop(0, hc // ROWS)
        def _(i):
            if nd == 2:
                total = wide(own[u, y, rsl(i), :]) + wide(xrecv[u, 0, rsl(i), :])
            else:
                total = wide(xrecv[u, 0, rsl(i), :])
                for e in range(1, nd):
                    total = total + wide(xrecv[u, e, rsl(i), :])
            yrecv[u, rsl(i), :] = (total * fac).astype(BF16)

        final_copy(a, q).start()

    def produce(a):
        left_all = cot if a == 0 else tok

        @pl.loop(0, nq)
        def _(q):
            u = a * nq + q
            slot = lax.rem(u, 2)

            @pl.when(u >= 2)
            def _():
                core_copy(u, slot).wait_send()

            for mine in range(2):
                for yy in range(2):
                    owner = yy * 2 + (c if mine else 1 - c)
                    feats = left_all[:, pl.ds(pl.multiple_of(owner * br, br), br)]
                    if a == 0:
                        tile = mm(feats, act[:, hsl(q)], 0, 0)
                    else:
                        tile = mm(dpre[:, hsl(q)], feats, 0, 0)
                    if mine:
                        own[u, yy] = tile.astype(BF16)
                    else:
                        psend[slot, yy] = tile.astype(BF16)
                if not mine:
                    core_copy(u, slot).start()

            @pl.when(u >= 1)
            def _():
                fold(u - 1)

            if a == 1:
                fold_rows(q)

    def out_copy(a, k):
        return send(osend.at[a, k - 1], orecv.at[a, k - 1], os_.at[a, k - 1], or_.at[a, k - 1], {"col": lax.rem(z + k, nz)})

    def terms(a):
        for k in range(1, nz + 1):
            to = lax.rem(z + k, nz)
            at = pl.ds(pl.multiple_of(to * bz, bz), bz)
            term = mm(act[...], wout[at, :], 1, 1) if a == 0 else mm(dpre[...], win[:, at], 1, 0)
            if k < nz:
                osend[a, k - 1] = term.astype(BF16)
                out_copy(a, k).start()
            else:
                mine_f32[a] = term

    for hook in hooks[nq:]:
        hook()
    zwait(1, nz - 2)
    lcopies(1)[0].wait()

    produce(0)
    weights_end(1)
    terms(0)

    @pl.loop(0, nq)
    def _(q):
        slope[:, hsl(q)] = slope[:, hsl(q)] * mm(cot[...], wout[:, hsl(q)], 1, 0)
        dpre[:, hsl(q)] = slope[:, hsl(q)].astype(BF16)

    terms(1)
    produce(1)
    fold(2 * nq - 1)

    total_units = 2 * nq

    def drain():
        @pl.loop(0, nq)
        def _(q):
            fold_rows(nq + q)
            finish(0, q)

    drain()

    def out_final(a):
        return pltpu.make_async_copy(orecv.at[a, 0], (out_ref, gtok_ref)[a], fin_sem.at[total_units + a])

    for a in range(2):
        for k in range(1, nz):
            out_copy(a, k).wait()

        @pl.loop(0, T // ROWS)
        def _(i):
            total = mine_f32[a, rsl(i), :]
            for k in range(1, nz):
                total = total + wide(orecv[a, k - 1, rsl(i), :])
            orecv[a, 0, rsl(i), :] = total.astype(BF16)

        out_final(a).start()

    @pl.loop(0, nq)
    def _(q):
        finish(1, q)

    for s in range(2):
        core_copy(total_units - 2 + s, (total_units - 2 + s) % 2).wait_send()

    for a in range(2):
        zdone(a)
        out_final(a).wait()

        @pl.loop(0, nq)
        def _(q):
            u = a * nq + q
            y_copy(u).wait_send()
            for k in range(1, nd):
                x_copy(u, k).wait_send()
            final_copy(a, q).wait()


def local(nz, nd, tokens, w_in, w_out, grad_out):
    T, bz = tokens.shape
    D = bz * nz
    H = w_in.shape[0]
    br = w_in.shape[1]
    hc = br
    nq = H // hc
    nx = 1 if nd == 2 else nd
    fac = 1.0 / math.sqrt(T * 4 * nd)
    dma = pltpu.SemaphoreType.DMA
    anyspec = pl.BlockSpec(memory_space=pl.ANY)
    flops = 12 * T * D * H
    return pl.pallas_call(
        functools.partial(kernel, nz, nd, fac),
        out_shape=(
            jax.ShapeDtypeStruct((T, bz), BF16),
            jax.ShapeDtypeStruct((T, bz), BF16),
            jax.ShapeDtypeStruct((H, br), BF16),
            jax.ShapeDtypeStruct((br, H), BF16),
        ),
        in_specs=[anyspec] * 4,
        out_specs=(anyspec,) * 4,
        scratch_shapes=[
            pltpu.VMEM((T, D), BF16),
            pltpu.VMEM((T, D), BF16),
            pltpu.VMEM((H, D), BF16),
            pltpu.VMEM((D, H), BF16),
            pltpu.VMEM((T, H), F32),
            pltpu.VMEM((T, H), BF16),
            pltpu.VMEM((T, H), BF16),
            pltpu.VMEM((2, 2, hc, br), BF16),
            pltpu.VMEM((2 * nq, 2, hc, br), BF16),
            pltpu.VMEM((2 * nq, 2, hc, br), BF16),
            pltpu.VMEM((2 * nq, hc, br), BF16),
            pltpu.VMEM((2 * nq, nx, hc, br), BF16),
            pltpu.VMEM((2, nz - 1, T, bz), BF16),
            pltpu.VMEM((2, nz - 1, T, bz), BF16),
            pltpu.VMEM((2, T, bz), F32),
            dma((2, 2)),
            dma((2, 2, nz - 1)),
            dma((2, 2, nz - 1)),
            dma((2, 1 + 2 * nd)),
            dma((2, 1 + 2 * nd)),
            dma((2,)),
            dma((2 * nq,)),
            dma((2 * nq,)),
            dma((2 * nq,)),
            dma((2 * nq, max(nd - 1, 1))),
            dma((2 * nq, max(nd - 1, 1))),
            dma((2, nz - 1)),
            dma((2, nz - 1)),
            dma((2 * nq + 2,)),
        ],
        compiler_params=pltpu.CompilerParams(
            collective_id=0, has_side_effects=True, vmem_limit_bytes=VMEM_LIMIT
        ),
        cost_estimate=pl.CostEstimate(flops=flops, bytes_accessed=20 * 2**20, transcendentals=2 * T * H),
        name="mlp",
    )(tokens, w_in, w_out, grad_out)


VMEM_LIMIT = 64 * 2**20 - 2**16


def solution(mesh):
    nz, nd = mesh.shape["col"], mesh.shape["depth"]
    in_specs = (
        P(("depth", "row"), "col"),
        P("col", "row"),
        P("row", "col"),
        P(("depth", "row"), "col"),
    )
    out_specs = (
        P(("depth", "row"), "col"),
        P(("depth", "row"), "col"),
        P("col", "row"),
        P("row", "col"),
    )
    return jax.shard_map(
        functools.partial(local, nz, nd), mesh=mesh, in_specs=in_specs, out_specs=out_specs, check_vma=False
    )
```

```python
import functools
import math

import jax
import jax.numpy as jnp
from jax import lax
from jax.experimental import pallas as pl
from jax.experimental.pallas import tpu as pltpu
from jax.sharding import PartitionSpec as P

F32 = jnp.float32
BF16 = jnp.bfloat16
MESH = pl.DeviceIdType.MESH
ROWS = 32


def mm(left, right, ldim, rdim):
    return lax.dot_general(
        left, right, (((ldim,), (rdim,)), ((), ())), preferred_element_type=F32
    )


def wide(x):
    return x.astype(F32)


def kernel(
    nz, nd, fac,
    tok_in, win_in, wout_in, cot_in,
    out_ref, gtok_ref, gwin_ref, gwout_ref,
    tok, cot, win, wout, slope, act, dpre,
    psend, own, crecv, yrecv, xrecv, osend, orecv, mine_f32,
    loc_sem, zs, zr, as_, ar, cs, cr, ys, yr, xs, xr, os_, or_, fin_sem,
):
    T, D = tok.shape
    H = win.shape[0]
    bz, br = D // nz, D // 4
    hr, hc = own.shape[2:]
    nq, ns = H // hc, hc // hr
    nu = nq * ns
    r = lax.axis_index("row")
    z = lax.axis_index("col")
    d = lax.axis_index("depth")
    c, y = lax.rem(r, 2), r // 2
    cp = y * 2 + (1 - c)
    yp = (1 - y) * 2 + c

    bar = pltpu.get_barrier_semaphore()
    for k in range(1, nz):
        pl.semaphore_signal(bar, inc=1, device_id={"col": lax.rem(z + k, nz)}, device_id_type=MESH)
    for k in range(1, nd):
        pl.semaphore_signal(bar, inc=1, device_id={"depth": lax.rem(d + k, nd)}, device_id_type=MESH)
    pl.semaphore_signal(bar, inc=1, device_id={"row": cp}, device_id_type=MESH)
    pl.semaphore_signal(bar, inc=1, device_id={"row": yp}, device_id_type=MESH)
    pl.semaphore_wait(bar, nz + nd)

    def send(src, dst, ss, rs, who):
        return pltpu.make_async_remote_copy(
            src_ref=src, dst_ref=dst, send_sem=ss, recv_sem=rs, device_id=who, device_id_type=MESH
        )

    def zcol(ref, i):
        return ref.at[:, pl.ds(pl.multiple_of(i * bz, bz), bz)]

    def wblk(a, i):
        at = pl.ds(pl.multiple_of(i * br, br), br)
        return win.at[:, at] if a == 0 else wout.at[at, :]

    acts_in, acts = (tok_in, cot_in), (tok, cot)
    w_in = (win_in, wout_in)

    def zhop(a, way, s):
        shard = z - s if way == 0 else z + s
        to = lax.rem(z + (1 if way == 0 else nz - 1), nz)
        src = acts_in[a] if s == 0 else zcol(acts[a], shard)
        return send(src, zcol(acts[a], shard), zs.at[a, way, s], zr.at[a, way, s], {"col": to})

    def sends(way, s):
        if way == 0:
            return jnp.logical_and(z >= s, z < nz - 1)
        return jnp.logical_and(z < nz - s, z > 0)

    def gets(way, s):
        return z >= s + 1 if way == 0 else z < nz - 1 - s

    def zstart(a, s):
        for way in range(2):
            pl.when(sends(way, s))(lambda way=way: zhop(a, way, s).start())

    def zwait(a, s):
        for way in range(2):
            pl.when(gets(way, s))(lambda way=way: zhop(a, way, s).wait_recv())

    def zdone(a):
        for s in range(nz - 1):
            for way in range(2):
                pl.when(sends(way, s))(lambda way=way, s=s: zhop(a, way, s).wait_send())

    def part(a, shard, e):
        if a == 0:
            n = H // nd
            return win.at[
                pl.ds(pl.multiple_of(e * n, n), n), pl.ds(pl.multiple_of(shard * br, br), br)
            ]
        n = br // nd
        return wout.at[pl.ds(pl.multiple_of(shard * br + e * n, n), n), :]

    def ycopy(a):
        n = (H if a == 0 else br) // nd
        src = w_in[a].at[pl.ds(pl.multiple_of(d * n, n), n), :]
        return send(src, part(a, r, d), as_.at[a, 0], ar.at[a, 0], {"row": yp})

    def ccopy(a):
        return send(w_in[a], wblk(a, r), as_.at[a, 1], ar.at[a, 1], {"row": cp})

    def dcopy(a, k):
        p = part(a, yp, d)
        return send(p, p, as_.at[a, 1 + k], ar.at[a, 1 + k], {"depth": lax.rem(d + k, nd)})

    def fcopy(a, k):
        p = part(a, yp, lax.rem(d + nd - k, nd))
        return send(p, p, as_.at[a, 1 + nd + k], ar.at[a, 1 + nd + k], {"row": cp})

    def lcopies(a):
        return (
            pltpu.make_async_copy(acts_in[a], zcol(acts[a], z), loc_sem.at[a, 0]),
            pltpu.make_async_copy(w_in[a], wblk(a, r), loc_sem.at[a, 1]),
        )

    def weights_hop(a):
        ycopy(a).wait_recv()
        for k in range(1, nd):
            dcopy(a, k).start()
        fcopy(a, 0).start()

    def weights_end(a):
        for k in range(1, nd):
            dcopy(a, k).wait_recv()
            fcopy(a, k).start()
        lcopies(a)[1].wait()
        ccopy(a).wait()
        ycopy(a).wait_send()
        for k in range(1, nd):
            dcopy(a, k).wait_send()
        for k in range(nd):
            fcopy(a, k).wait()

    ycopy(0).start()
    zstart(0, 0)
    for a in range(2):
        ccopy(a).start()
        for x in lcopies(a):
            x.start()
    zwait(0, 0)
    if nz > 2:
        zstart(0, 1)
    weights_hop(0)
    ycopy(1).start()
    for s in range(2, nz - 1):
        zwait(0, s - 1)
        zstart(0, s)
    zstart(1, 0)
    if nz > 2:
        zwait(0, nz - 2)
    lcopies(0)[0].wait()
    weights_end(0)

    def cot_hop(s):
        zwait(1, s - 1)
        zstart(1, s)

    hooks = [functools.partial(cot_hop, s) for s in range(1, nz - 1)]
    hooks.insert(1, functools.partial(weights_hop, 1))

    def hsl(q):
        return pl.ds(pl.multiple_of(q * hc, hc), hc)

    def rsl(i):
        return pl.ds(pl.multiple_of(i * ROWS, ROWS), ROWS)

    @pl.loop(0, nq)
    def _(q):
        for i, hook in enumerate(hooks[:nq]):
            pl.when(q == i)(hook)
        slope[:, hsl(q)] = mm(tok[...], win[hsl(q), :], 1, 1)

        @pl.loop(0, T // ROWS)
        def _(i):
            v = slope[rsl(i), hsl(q)]
            half = 0.5 * (1.0 + lax.erf(v * (1.0 / math.sqrt(2.0))))
            act[rsl(i), hsl(q)] = (v * half).astype(BF16)
            slope[rsl(i), hsl(q)] = half + v * jnp.exp(-0.5 * v * v) * (1.0 / math.sqrt(2.0 * math.pi))

    def core_copy(u, slot):
        return send(psend.at[slot], crecv.at[u], cs.at[slot], cr.at[u], {"row": cp})

    def y_copy(u):
        return send(own.at[u, 1 - y], yrecv.at[u], ys.at[u], yr.at[u], {"row": yp})

    def ufinal(u):
        return own.at[u, y] if nd == 2 else xrecv.at[u, d]

    def x_copy(u, k):
        dst = xrecv.at[u, 0] if nd == 2 else xrecv.at[u, d]
        return send(ufinal(u), dst, xs.at[u, k - 1], xr.at[u, k - 1], {"depth": lax.rem(d + k, nd)})

    def fold(u):
        core_copy(u, lax.rem(u, 2)).wait_recv()

        @pl.loop(0, hr // ROWS)
        def _(i):
            own[u, 1 - y, rsl(i), :] = (
                wide(own[u, 1 - y, rsl(i), :]) + wide(crecv[u, 1 - y, rsl(i), :])
            ).astype(BF16)

        y_copy(u).start()

    def fold_rows(u):
        y_copy(u).wait_recv()
        dst = ufinal(u)

        @pl.loop(0, hr // ROWS)
        def _(i):
            dst[rsl(i), :] = (
                wide(own[u, y, rsl(i), :]) + wide(crecv[u, y, rsl(i), :]) + wide(yrecv[u, rsl(i), :])
            ).astype(BF16)

        for k in range(1, nd):
            x_copy(u, k).start()

    def rows_at(w):
        return pl.ds(pl.multiple_of(w * hr, hr), hr)

    def final_copy(a, w):
        u = a * nu + w
        if a == 0:
            dst = gwout_ref.at[rows_at(lax.rem(w, ns)), hsl(w // ns)]
        else:
            dst = gwin_ref.at[rows_at(w), :]
        return pltpu.make_async_copy(yrecv.at[u], dst, fin_sem.at[u])

    def finish(a, w):
        u = a * nu + w
        for k in range(1, nd):
            x_copy(u, k).wait_recv()

        @pl.loop(0, hr // ROWS)
        def _(i):
            if nd == 2:
                total = wide(own[u, y, rsl(i), :]) + wide(xrecv[u, 0, rsl(i), :])
            else:
                total = wide(xrecv[u, 0, rsl(i), :])
                for e in range(1, nd):
                    total = total + wide(xrecv[u, e, rsl(i), :])
            yrecv[u, rsl(i), :] = (total * fac).astype(BF16)

        final_copy(a, w).start()

    def produce(a):
        @pl.loop(0, nu)
        def _(w):
            u = a * nu + w
            slot = lax.rem(u, 2)

            @pl.when(u >= 2)
            def _():
                core_copy(u, slot).wait_send()

            for mine in range(2):
                for yy in range(2):
                    owner = yy * 2 + (c if mine else 1 - c)
                    if a == 0:
                        base = owner * br + lax.rem(w, ns) * hr
                        feats = cot[:, pl.ds(pl.multiple_of(base, hr), hr)]
                        tile = mm(feats, act[:, hsl(w // ns)], 0, 0)
                    else:
                        feats = tok[:, pl.ds(pl.multiple_of(owner * br, br), br)]
                        tile = mm(dpre[:, rows_at(w)], feats, 0, 0)
                    if mine:
                        own[u, yy] = tile.astype(BF16)
                    else:
                        psend[slot, yy] = tile.astype(BF16)
                if not mine:
                    core_copy(u, slot).start()

            @pl.when(w >= 1)
            def _():
                fold(u - 1)

            if a == 1:
                for i, j in enumerate(range(cuts[3], nu)):
                    pl.when(w == min(1 + 4 * i, nu - 1))(functools.partial(fold_rows, j))

        fold(a * nu + nu - 1)

    def out_copy(a, k):
        return send(osend.at[a, k - 1], orecv.at[a, k - 1], os_.at[a, k - 1], or_.at[a, k - 1], {"col": lax.rem(z + k, nz)})

    def terms(a):
        for k in range(1, nz + 1):
            to = lax.rem(z + k, nz)
            at = pl.ds(pl.multiple_of(to * bz, bz), bz)
            term = mm(act[...], wout[at, :], 1, 1) if a == 0 else mm(dpre[...], win[:, at], 1, 0)
            if k < nz:
                osend[a, k - 1] = term.astype(BF16)
                out_copy(a, k).start()
            else:
                mine_f32[a] = term

    for hook in hooks[nq:]:
        hook()
    zwait(1, nz - 2)
    lcopies(1)[0].wait()

    cuts = (nu // 4, 3 * nu // 8, 5 * nu // 8, 6 * nu // 8)
    produce(0)
    for j in range(cuts[0]):
        fold_rows(j)
    weights_end(1)
    terms(0)
    for j in range(cuts[0], cuts[1]):
        fold_rows(j)

    @pl.loop(0, nq)
    def _(q):
        slope[:, hsl(q)] = slope[:, hsl(q)] * mm(cot[...], wout[:, hsl(q)], 1, 0)
        dpre[:, hsl(q)] = slope[:, hsl(q)].astype(BF16)

    for j in range(cuts[1], cuts[2]):
        fold_rows(j)
    terms(1)
    for j in range(cuts[2], cuts[3]):
        fold_rows(j)
    produce(1)

    total_units = 2 * nu

    def drain():
        @pl.loop(0, nu)
        def _(w):
            fold_rows(nu + w)
            finish(0, w)

    drain()

    def out_final(a):
        return pltpu.make_async_copy(orecv.at[a, 0], (out_ref, gtok_ref)[a], fin_sem.at[total_units + a])

    for a in range(2):
        for k in range(1, nz):
            out_copy(a, k).wait()

        @pl.loop(0, T // ROWS)
        def _(i):
            total = mine_f32[a, rsl(i), :]
            for k in range(1, nz):
                total = total + wide(orecv[a, k - 1, rsl(i), :])
            orecv[a, 0, rsl(i), :] = total.astype(BF16)

        out_final(a).start()

    @pl.loop(0, nu)
    def _(w):
        finish(1, w)

    for s in range(2):
        core_copy(total_units - 2 + s, (total_units - 2 + s) % 2).wait_send()

    for a in range(2):
        zdone(a)
        out_final(a).wait()

        @pl.loop(0, nu)
        def _(w):
            u = a * nu + w
            y_copy(u).wait_send()
            for k in range(1, nd):
                x_copy(u, k).wait_send()
            final_copy(a, w).wait()


def local(nz, nd, tokens, w_in, w_out, grad_out):
    T, bz = tokens.shape
    D = bz * nz
    H = w_in.shape[0]
    br = w_in.shape[1]
    hc = br
    hr = hc // 2
    nu = 2 * (H // hc)
    nx = 1 if nd == 2 else nd
    fac = 1.0 / math.sqrt(T * 4 * nd)
    dma = pltpu.SemaphoreType.DMA
    anyspec = pl.BlockSpec(memory_space=pl.ANY)
    flops = 12 * T * D * H
    return pl.pallas_call(
        functools.partial(kernel, nz, nd, fac),
        out_shape=(
            jax.ShapeDtypeStruct((T, bz), BF16),
            jax.ShapeDtypeStruct((T, bz), BF16),
            jax.ShapeDtypeStruct((H, br), BF16),
            jax.ShapeDtypeStruct((br, H), BF16),
        ),
        in_specs=[anyspec] * 4,
        out_specs=(anyspec,) * 4,
        scratch_shapes=[
            pltpu.VMEM((T, D), BF16),
            pltpu.VMEM((T, D), BF16),
            pltpu.VMEM((H, D), BF16),
            pltpu.VMEM((D, H), BF16),
            pltpu.VMEM((T, H), F32),
            pltpu.VMEM((T, H), BF16),
            pltpu.VMEM((T, H), BF16),
            pltpu.VMEM((2, 2, hr, br), BF16),
            pltpu.VMEM((2 * nu, 2, hr, br), BF16),
            pltpu.VMEM((2 * nu, 2, hr, br), BF16),
            pltpu.VMEM((2 * nu, hr, br), BF16),
            pltpu.VMEM((2 * nu, nx, hr, br), BF16),
            pltpu.VMEM((2, nz - 1, T, bz), BF16),
            pltpu.VMEM((2, nz - 1, T, bz), BF16),
            pltpu.VMEM((2, T, bz), F32),
            dma((2, 2)),
            dma((2, 2, nz - 1)),
            dma((2, 2, nz - 1)),
            dma((2, 1 + 2 * nd)),
            dma((2, 1 + 2 * nd)),
            dma((2,)),
            dma((2 * nu,)),
            dma((2 * nu,)),
            dma((2 * nu,)),
            dma((2 * nu, max(nd - 1, 1))),
            dma((2 * nu, max(nd - 1, 1))),
            dma((2, nz - 1)),
            dma((2, nz - 1)),
            dma((2 * nu + 2,)),
        ],
        compiler_params=pltpu.CompilerParams(
            collective_id=0, has_side_effects=True, vmem_limit_bytes=VMEM_LIMIT
        ),
        cost_estimate=pl.CostEstimate(flops=flops, bytes_accessed=20 * 2**20, transcendentals=2 * T * H),
        name="mlp",
    )(tokens, w_in, w_out, grad_out)


VMEM_LIMIT = 64 * 2**20 - 2**16


def solution(mesh):
    nz, nd = mesh.shape["col"], mesh.shape["depth"]
    in_specs = (
        P(("depth", "row"), "col"),
        P("col", "row"),
        P("row", "col"),
        P(("depth", "row"), "col"),
    )
    out_specs = (
        P(("depth", "row"), "col"),
        P(("depth", "row"), "col"),
        P("col", "row"),
        P("row", "col"),
    )
    return jax.shard_map(
        functools.partial(local, nz, nd), mesh=mesh, in_specs=in_specs, out_specs=out_specs, check_vma=False
    )
```

```python
import functools
import math

import jax
import jax.numpy as jnp
from jax import lax
from jax.experimental import pallas as pl
from jax.experimental.pallas import tpu as pltpu
from jax.sharding import PartitionSpec as P

F32 = jnp.float32
BF16 = jnp.bfloat16
MESH = pl.DeviceIdType.MESH
ROWS = 32


def mm(left, right, ldim, rdim):
    return lax.dot_general(
        left, right, (((ldim,), (rdim,)), ((), ())), preferred_element_type=F32
    )


def wide(x):
    return x.astype(F32)


def kernel(
    nz, nd, fac,
    tok_in, win_in, wout_in, cot_in,
    out_ref, gtok_ref, gwin_ref, gwout_ref,
    tok, cot, win, wout, slope, act, dpre,
    psend, own, crecv, yrecv, xrecv, osend, orecv, mine_f32,
    loc_sem, zs, zr, as_, ar, cs, cr, ys, yr, xs, xr, os_, or_, fin_sem,
):
    T, D = tok.shape
    H = win.shape[0]
    bz, br = D // nz, D // 4
    hr, hc = own.shape[2:]
    nq, ns = H // hc, hc // hr
    nu = nq * ns
    r = lax.axis_index("row")
    z = lax.axis_index("col")
    d = lax.axis_index("depth")
    c, y = lax.rem(r, 2), r // 2
    cp = y * 2 + (1 - c)
    yp = (1 - y) * 2 + c

    bar = pltpu.get_barrier_semaphore()
    for k in range(1, nz):
        pl.semaphore_signal(bar, inc=1, device_id={"col": lax.rem(z + k, nz)}, device_id_type=MESH)
    for k in range(1, nd):
        pl.semaphore_signal(bar, inc=1, device_id={"depth": lax.rem(d + k, nd)}, device_id_type=MESH)
    pl.semaphore_signal(bar, inc=1, device_id={"row": cp}, device_id_type=MESH)
    pl.semaphore_signal(bar, inc=1, device_id={"row": yp}, device_id_type=MESH)
    pl.semaphore_wait(bar, nz + nd)

    def send(src, dst, ss, rs, who):
        return pltpu.make_async_remote_copy(
            src_ref=src, dst_ref=dst, send_sem=ss, recv_sem=rs, device_id=who, device_id_type=MESH
        )

    def zcol(ref, i):
        return ref.at[:, pl.ds(pl.multiple_of(i * bz, bz), bz)]

    def wblk(a, i):
        at = pl.ds(pl.multiple_of(i * br, br), br)
        return win.at[:, at] if a == 0 else wout.at[at, :]

    acts_in, acts = (tok_in, cot_in), (tok, cot)
    w_in = (win_in, wout_in)

    def zhop(a, way, s):
        shard = z - s if way == 0 else z + s
        to = lax.rem(z + (1 if way == 0 else nz - 1), nz)
        src = acts_in[a] if s == 0 else zcol(acts[a], shard)
        return send(src, zcol(acts[a], shard), zs.at[a, way, s], zr.at[a, way, s], {"col": to})

    def sends(way, s):
        if way == 0:
            return jnp.logical_and(z >= s, z < nz - 1)
        return jnp.logical_and(z < nz - s, z > 0)

    def gets(way, s):
        return z >= s + 1 if way == 0 else z < nz - 1 - s

    def zstart(a, s):
        for way in range(2):
            pl.when(sends(way, s))(lambda way=way: zhop(a, way, s).start())

    def zwait(a, s):
        for way in range(2):
            pl.when(gets(way, s))(lambda way=way: zhop(a, way, s).wait_recv())

    def zdone(a):
        for s in range(nz - 1):
            for way in range(2):
                pl.when(sends(way, s))(lambda way=way, s=s: zhop(a, way, s).wait_send())

    def part(a, shard, e):
        if a == 0:
            n = H // nd
            return win.at[
                pl.ds(pl.multiple_of(e * n, n), n), pl.ds(pl.multiple_of(shard * br, br), br)
            ]
        n = br // nd
        return wout.at[pl.ds(pl.multiple_of(shard * br + e * n, n), n), :]

    def ycopy(a):
        n = (H if a == 0 else br) // nd
        src = w_in[a].at[pl.ds(pl.multiple_of(d * n, n), n), :]
        return send(src, part(a, r, d), as_.at[a, 0], ar.at[a, 0], {"row": yp})

    def ccopy(a):
        return send(w_in[a], wblk(a, r), as_.at[a, 1], ar.at[a, 1], {"row": cp})

    def dcopy(a, k):
        p = part(a, yp, d)
        return send(p, p, as_.at[a, 1 + k], ar.at[a, 1 + k], {"depth": lax.rem(d + k, nd)})

    def fcopy(a, k):
        p = part(a, yp, lax.rem(d + nd - k, nd))
        return send(p, p, as_.at[a, 1 + nd + k], ar.at[a, 1 + nd + k], {"row": cp})

    def lcopies(a):
        return (
            pltpu.make_async_copy(acts_in[a], zcol(acts[a], z), loc_sem.at[a, 0]),
            pltpu.make_async_copy(w_in[a], wblk(a, r), loc_sem.at[a, 1]),
        )

    def weights_hop(a):
        ycopy(a).wait_recv()
        for k in range(1, nd):
            dcopy(a, k).start()
        fcopy(a, 0).start()

    def weights_end(a):
        for k in range(1, nd):
            dcopy(a, k).wait_recv()
            fcopy(a, k).start()
        lcopies(a)[1].wait()
        ccopy(a).wait()
        ycopy(a).wait_send()
        for k in range(1, nd):
            dcopy(a, k).wait_send()
        for k in range(nd):
            fcopy(a, k).wait()

    ycopy(0).start()
    zstart(0, 0)
    for a in range(2):
        ccopy(a).start()
        for x in lcopies(a):
            x.start()
    zwait(0, 0)
    if nz > 2:
        zstart(0, 1)
    weights_hop(0)
    ycopy(1).start()
    for s in range(2, nz - 1):
        zwait(0, s - 1)
        zstart(0, s)
    zstart(1, 0)
    if nz > 2:
        zwait(0, nz - 2)
    lcopies(0)[0].wait()
    weights_end(0)

    def cot_hop(s):
        zwait(1, s - 1)
        zstart(1, s)

    hooks = [functools.partial(cot_hop, s) for s in range(1, nz - 1)]
    hooks.insert(1, functools.partial(weights_hop, 1))

    def hsl(q):
        return pl.ds(pl.multiple_of(q * hc, hc), hc)

    def rsl(i):
        return pl.ds(pl.multiple_of(i * ROWS, ROWS), ROWS)

    @pl.loop(0, nq)
    def _(q):
        for i, hook in enumerate(hooks[:nq]):
            pl.when(q == i)(hook)
        slope[:, hsl(q)] = mm(tok[...], win[hsl(q), :], 1, 1)

        @pl.loop(0, T // ROWS)
        def _(i):
            v = slope[rsl(i), hsl(q)]
            half = 0.5 * (1.0 + lax.erf(v * (1.0 / math.sqrt(2.0))))
            act[rsl(i), hsl(q)] = (v * half).astype(BF16)
            slope[rsl(i), hsl(q)] = half + v * jnp.exp(-0.5 * v * v) * (1.0 / math.sqrt(2.0 * math.pi))

    def core_copy(u, slot):
        return send(psend.at[slot], crecv.at[u], cs.at[slot], cr.at[u], {"row": cp})

    def y_copy(u):
        return send(own.at[u, 1 - y], yrecv.at[u], ys.at[u], yr.at[u], {"row": yp})

    def ufinal(u):
        return own.at[u, y] if nd == 2 else xrecv.at[u, d]

    def x_copy(u, k):
        dst = xrecv.at[u, 0] if nd == 2 else xrecv.at[u, d]
        return send(ufinal(u), dst, xs.at[u, k - 1], xr.at[u, k - 1], {"depth": lax.rem(d + k, nd)})

    def fold(u):
        core_copy(u, lax.rem(u, 2)).wait_recv()

        @pl.loop(0, hr // ROWS)
        def _(i):
            own[u, 1 - y, rsl(i), :] = (
                wide(own[u, 1 - y, rsl(i), :]) + wide(crecv[u, 1 - y, rsl(i), :])
            ).astype(BF16)

        y_copy(u).start()

    def fold_rows(u):
        y_copy(u).wait_recv()
        dst = ufinal(u)

        @pl.loop(0, hr // ROWS)
        def _(i):
            dst[rsl(i), :] = (
                wide(own[u, y, rsl(i), :]) + wide(crecv[u, y, rsl(i), :]) + wide(yrecv[u, rsl(i), :])
            ).astype(BF16)

        for k in range(1, nd):
            x_copy(u, k).start()

    def rows_at(w):
        return pl.ds(pl.multiple_of(w * hr, hr), hr)

    def final_copy(a, w):
        u = a * nu + w
        if a == 0:
            dst = gwout_ref.at[rows_at(lax.rem(w, ns)), hsl(w // ns)]
        else:
            dst = gwin_ref.at[rows_at(w), :]
        return pltpu.make_async_copy(yrecv.at[u], dst, fin_sem.at[u])

    def finish(a, w):
        u = a * nu + w
        for k in range(1, nd):
            x_copy(u, k).wait_recv()

        @pl.loop(0, hr // ROWS)
        def _(i):
            if nd == 2:
                total = wide(own[u, y, rsl(i), :]) + wide(xrecv[u, 0, rsl(i), :])
            else:
                total = wide(xrecv[u, 0, rsl(i), :])
                for e in range(1, nd):
                    total = total + wide(xrecv[u, e, rsl(i), :])
            yrecv[u, rsl(i), :] = (total * fac).astype(BF16)

        final_copy(a, w).start()

    def produce(a):
        @pl.loop(0, nu)
        def _(w):
            u = a * nu + w
            slot = lax.rem(u, 2)

            @pl.when(u >= 2)
            def _():
                core_copy(u, slot).wait_send()

            for mine in range(2):
                for yy in range(2):
                    owner = yy * 2 + (c if mine else 1 - c)
                    if a == 0:
                        base = owner * br + lax.rem(w, ns) * hr
                        feats = cot[:, pl.ds(pl.multiple_of(base, hr), hr)]
                        tile = mm(feats, act[:, hsl(w // ns)], 0, 0)
                    else:
                        feats = tok[:, pl.ds(pl.multiple_of(owner * br, br), br)]
                        tile = mm(dpre[:, rows_at(w)], feats, 0, 0)
                    if mine:
                        own[u, yy] = tile.astype(BF16)
                    else:
                        psend[slot, yy] = tile.astype(BF16)
                if not mine:
                    core_copy(u, slot).start()

            @pl.when(w >= 1)
            def _():
                fold(u - 1)

            if a == 1:
                for i, j in enumerate(range(cuts[3], nu)):
                    pl.when(w == min(1 + 2 * i, nu - 1))(functools.partial(fold_rows, j))

        fold(a * nu + nu - 1)

    def out_copy(a, k):
        return send(osend.at[a, k - 1], orecv.at[a, k - 1], os_.at[a, k - 1], or_.at[a, k - 1], {"col": lax.rem(z + k, nz)})

    def terms(a):
        for k in range(1, nz + 1):
            to = lax.rem(z + k, nz)
            at = pl.ds(pl.multiple_of(to * bz, bz), bz)
            term = mm(act[...], wout[at, :], 1, 1) if a == 0 else mm(dpre[...], win[:, at], 1, 0)
            if k < nz:
                osend[a, k - 1] = term.astype(BF16)
                out_copy(a, k).start()
            else:
                mine_f32[a] = term

    for hook in hooks[nq:]:
        hook()
    zwait(1, nz - 2)
    lcopies(1)[0].wait()

    cuts = (nu // 8, nu // 4, 3 * nu // 8, nu // 2)
    produce(0)
    for j in range(cuts[0]):
        fold_rows(j)
    weights_end(1)
    terms(0)
    for j in range(cuts[0], cuts[1]):
        fold_rows(j)

    @pl.loop(0, nq)
    def _(q):
        slope[:, hsl(q)] = slope[:, hsl(q)] * mm(cot[...], wout[:, hsl(q)], 1, 0)
        dpre[:, hsl(q)] = slope[:, hsl(q)].astype(BF16)

    for j in range(cuts[1], cuts[2]):
        fold_rows(j)
    terms(1)
    for j in range(cuts[2], cuts[3]):
        fold_rows(j)
    produce(1)

    total_units = 2 * nu

    def drain():
        @pl.loop(0, nu)
        def _(w):
            fold_rows(nu + w)
            finish(0, w)

    drain()

    def out_final(a):
        return pltpu.make_async_copy(orecv.at[a, 0], (out_ref, gtok_ref)[a], fin_sem.at[total_units + a])

    for a in range(2):
        for k in range(1, nz):
            out_copy(a, k).wait()

        @pl.loop(0, T // ROWS)
        def _(i):
            total = mine_f32[a, rsl(i), :]
            for k in range(1, nz):
                total = total + wide(orecv[a, k - 1, rsl(i), :])
            orecv[a, 0, rsl(i), :] = total.astype(BF16)

        out_final(a).start()

    @pl.loop(0, nu)
    def _(w):
        finish(1, w)

    for s in range(2):
        core_copy(total_units - 2 + s, (total_units - 2 + s) % 2).wait_send()

    for a in range(2):
        zdone(a)
        out_final(a).wait()

        @pl.loop(0, nu)
        def _(w):
            u = a * nu + w
            y_copy(u).wait_send()
            for k in range(1, nd):
                x_copy(u, k).wait_send()
            final_copy(a, w).wait()


def local(nz, nd, tokens, w_in, w_out, grad_out):
    T, bz = tokens.shape
    D = bz * nz
    H = w_in.shape[0]
    br = w_in.shape[1]
    hc = br
    hr = hc // 2
    nu = 2 * (H // hc)
    nx = 1 if nd == 2 else nd
    fac = 1.0 / math.sqrt(T * 4 * nd)
    dma = pltpu.SemaphoreType.DMA
    anyspec = pl.BlockSpec(memory_space=pl.ANY)
    flops = 12 * T * D * H
    return pl.pallas_call(
        functools.partial(kernel, nz, nd, fac),
        out_shape=(
            jax.ShapeDtypeStruct((T, bz), BF16),
            jax.ShapeDtypeStruct((T, bz), BF16),
            jax.ShapeDtypeStruct((H, br), BF16),
            jax.ShapeDtypeStruct((br, H), BF16),
        ),
        in_specs=[anyspec] * 4,
        out_specs=(anyspec,) * 4,
        scratch_shapes=[
            pltpu.VMEM((T, D), BF16),
            pltpu.VMEM((T, D), BF16),
            pltpu.VMEM((H, D), BF16),
            pltpu.VMEM((D, H), BF16),
            pltpu.VMEM((T, H), F32),
            pltpu.VMEM((T, H), BF16),
            pltpu.VMEM((T, H), BF16),
            pltpu.VMEM((2, 2, hr, br), BF16),
            pltpu.VMEM((2 * nu, 2, hr, br), BF16),
            pltpu.VMEM((2 * nu, 2, hr, br), BF16),
            pltpu.VMEM((2 * nu, hr, br), BF16),
            pltpu.VMEM((2 * nu, nx, hr, br), BF16),
            pltpu.VMEM((2, nz - 1, T, bz), BF16),
            pltpu.VMEM((2, nz - 1, T, bz), BF16),
            pltpu.VMEM((2, T, bz), F32),
            dma((2, 2)),
            dma((2, 2, nz - 1)),
            dma((2, 2, nz - 1)),
            dma((2, 1 + 2 * nd)),
            dma((2, 1 + 2 * nd)),
            dma((2,)),
            dma((2 * nu,)),
            dma((2 * nu,)),
            dma((2 * nu,)),
            dma((2 * nu, max(nd - 1, 1))),
            dma((2 * nu, max(nd - 1, 1))),
            dma((2, nz - 1)),
            dma((2, nz - 1)),
            dma((2 * nu + 2,)),
        ],
        compiler_params=pltpu.CompilerParams(
            collective_id=0, has_side_effects=True, vmem_limit_bytes=VMEM_LIMIT
        ),
        cost_estimate=pl.CostEstimate(flops=flops, bytes_accessed=20 * 2**20, transcendentals=2 * T * H),
        name="mlp",
    )(tokens, w_in, w_out, grad_out)


VMEM_LIMIT = 64 * 2**20 - 2**16


def solution(mesh):
    nz, nd = mesh.shape["col"], mesh.shape["depth"]
    in_specs = (
        P(("depth", "row"), "col"),
        P("col", "row"),
        P("row", "col"),
        P(("depth", "row"), "col"),
    )
    out_specs = (
        P(("depth", "row"), "col"),
        P(("depth", "row"), "col"),
        P("col", "row"),
        P("row", "col"),
    )
    return jax.shard_map(
        functools.partial(local, nz, nd), mesh=mesh, in_specs=in_specs, out_specs=out_specs, check_vma=False
    )
```
